32 devices in a mesh: sub: 16 (over z, y, x), face: 2 (over core).
Axes of the slice: x: 2, y: 2, z: 4, core: 2. Of those that a mesh axis runs over, the one named last changes fastest.
Arguments:
- schur_blocks: float32 [16, 1024, 1024], P('sub', 'face'), may hold values from -1 to 4, as said below
- rigid_body_modes: float32 [16, 6, 1024], P('sub', None, 'face'), may hold values from -1 to 1
- load_cases: float32 [16, 1024, 128], P('sub', 'face'), may hold values from -60 to 60
- face_sizes: int32 [16, 4], P('sub', 'face'), may hold values from 128 to 256
- contact_mask: int32 [16, 1024], P('sub', 'face'), may hold values 0 or 1
- friction_mask: int32 [16, 1024], P('sub', 'face'), may hold values 0 or 1
- cluster_ids: int32 [16], P('sub'), may hold values from 0 to 1, as said below
- pairing: int32 [16, 2, 2, 1], P('sub', 'face'), may hold values from 0 to 0, as said below
Outputs:
- multipliers: float32 [16, 1024, 128], P('sub', 'face')
- residual: float32 [16, 1024, 128], P('sub', 'face')
The draws below stay inside these ranges and needn't reach their ends.
Inputs may be any that keep to these rules, and one draw needn't show every extreme that they name: `schur_blocks`: each block is symmetric and positive definite. `cluster_ids`: every cluster number names exactly 8 subdomains. Each device holds one subdomain, so every pairing entry is 0 (the identity matching); pairing[(i + 1) mod 16, c, 1, pairing[i, c, 0, g]] = g holds trivially.
All inputs are finite; a program needn't handle non-finite values. No bound on the sum of `contact_mask` or of `friction_mask` on one device may be relied on, other than what follows from the above.
Results may differ from the reference program's by a relative error of at most 0.00025.
Values sent between devices are 32-bit elements; how exact they have to be, the bound alone decides.
A program may use at most 64 MiB of HBM per device.

```python
import jax
import jax.numpy as jnp
from jax import lax

SUB_DEV = 1
NRHS = 128
FS = 256
NF = 4
MODES = 6
ITERS = 2
DS = 1024
GROUPS = 16
SUBS = 16
CLUSTERS = 2


def rigid_draw(key):
    key_order = jax.random.fold_in(key, 11)
    key_modes = jax.random.fold_in(key, 12)
    key_coef = jax.random.fold_in(key, 13)
    scores = jax.random.randint(key_order, (SUBS,), 0, 1 << 16) * SUBS + jnp.arange(SUBS, dtype=jnp.int32)
    order = jnp.argsort(scores)
    cluster = (jnp.argsort(order) // 8).astype(jnp.int32)
    modes = jax.random.truncated_normal(key_modes, -3.0, 3.0, (SUBS, MODES, DS), jnp.float32)
    modes = modes / DS ** 0.5
    coef = jax.random.truncated_normal(key_coef, -3.0, 3.0, (CLUSTERS, MODES, NRHS), jnp.float32) * 6.0
    return (cluster, modes, coef)


def draw_cluster_ids(key, part):
    return rigid_draw(key)[0]


def draw_rigid_body_modes(key, part):
    return rigid_draw(key)[1]


def draw_load_cases(key, part):
    cluster, modes, coef = rigid_draw(key)
    key_noise = jax.random.fold_in(key, 14)
    scatter_copies = coef[cluster]
    smooth_part = jnp.einsum('smk,smr->skr', modes, scatter_copies)
    noise = jax.random.truncated_normal(key_noise, -3.0, 3.0, (SUBS, DS, NRHS), jnp.float32)
    return smooth_part + noise


def draw_schur_blocks(key, part):
    key_noise = jax.random.fold_in(key, 21)
    key_diag = jax.random.fold_in(key, 22)
    entries = jax.random.truncated_normal(key_noise, -3.0, 3.0, (SUBS, DS, DS), jnp.float32)
    scaled = entries * (0.5 / DS ** 0.5)
    symmetric = (scaled + jnp.swapaxes(scaled, 1, 2)) * 0.7071
    diagonal = jnp.exp(jax.random.uniform(key_diag, (SUBS, DS), jnp.float32, jnp.log(1.5), jnp.log(3.0)))
    return symmetric + diagonal[:, :, None] * jnp.eye(DS, dtype=jnp.float32)[None]


def draw_pairing(key, part):
    scores = jax.random.randint(key, (GROUPS, 2, SUB_DEV), 0, 1 << 16) * SUB_DEV + jnp.arange(SUB_DEV, dtype=jnp.int32)
    forward = jnp.argsort(scores, axis=-1).astype(jnp.int32)
    backward = jnp.argsort(jnp.roll(forward, 1, axis=0), axis=-1).astype(jnp.int32)
    return jnp.stack([forward, backward], axis=2)


def with_ends(values, stream_key, smallest, largest):
    longest = values.shape.index(max(values.shape))
    spots = []
    for shift in (0, 1):
        where = [jax.random.randint(jax.random.fold_in(stream_key, axis), (), 0, length) for axis, length in enumerate(values.shape)]
        where[longest] = (where[longest] + shift) % values.shape[longest]
        spots.append(tuple(where))
    return values.at[spots[0]].set(smallest).at[spots[1]].set(largest)


def setup_inputs(seed: int = 0) -> dict:
    seeds = jax.random.split(jax.random.key(seed), 9)
    return {
        "schur_blocks": draw_schur_blocks(jax.random.fold_in(seeds[8], 71), 0),
        "rigid_body_modes": draw_rigid_body_modes(jax.random.fold_in(seeds[8], 71), 0),
        "load_cases": draw_load_cases(jax.random.fold_in(seeds[8], 71), 0),
        "face_sizes": with_ends(jax.random.randint(seeds[3], (SUBS, NF), FS // 2, FS + 1), jax.random.fold_in(seeds[3], 1), FS // 2, FS).astype(jnp.int32),
        "contact_mask": with_ends((jax.random.randint(seeds[4], (SUBS, DS), 0, 3) < 1).astype(jnp.int32), jax.random.fold_in(seeds[4], 1), 0, 1),
        "friction_mask": with_ends((jax.random.randint(seeds[5], (SUBS, DS), 0, 2) < 1).astype(jnp.int32), jax.random.fold_in(seeds[5], 1), 0, 1),
        "cluster_ids": draw_cluster_ids(jax.random.fold_in(seeds[8], 71), 0),
        "pairing": draw_pairing(jax.random.fold_in(seeds[8], 71), 0),
    }


HIGH_ACCURACY = lax.Precision.HIGHEST

def partner_of(entry_values, pairing):
    groups = pairing.shape[0]
    per_group = pairing.shape[3]
    sub_ids = jnp.arange(groups * per_group, dtype=jnp.int32)
    group_ids = sub_ids // per_group
    local_ids = sub_ids % per_group
    face_ids = jnp.arange(NF, dtype=jnp.int32)
    face_half = face_ids // 2
    face_side = face_ids % 2
    shift_step = (1 - 2 * face_side).astype(jnp.int32)
    neighbour = (group_ids[:, None] + shift_step[None, :]) % groups
    chosen = pairing[group_ids[:, None], face_half[None, :], face_side[None, :], local_ids[:, None]]
    source = (neighbour * per_group + chosen).astype(jnp.int32)
    source_face = (face_ids + shift_step).astype(jnp.int32)
    return entry_values[source, source_face[None, :]]

def coarse_inverse(coarse_gram):
    lower_factor = jnp.linalg.cholesky(coarse_gram)
    eye_block = jnp.broadcast_to(jnp.eye(coarse_gram.shape[1], dtype=coarse_gram.dtype), coarse_gram.shape)
    inverse_factor = lax.linalg.triangular_solve(lower_factor, eye_block, left_side=True, lower=True)
    return jnp.einsum('bkm,bkn->bmn', inverse_factor, inverse_factor, precision=HIGH_ACCURACY)

def project(entry_values, rigid_body_modes, choice_matrix, inverse):
    subdomain_part = jnp.einsum('smk,skr->smr', rigid_body_modes, entry_values, precision=HIGH_ACCURACY)
    coarse = jnp.einsum('sb,smr->bmr', choice_matrix, subdomain_part, precision=HIGH_ACCURACY)
    weight_factors = jnp.einsum('bmn,bnr->bmr', inverse, coarse, precision=HIGH_ACCURACY)
    scatter_copies = jnp.einsum('sb,bmr->smr', choice_matrix, weight_factors, precision=HIGH_ACCURACY)
    return entry_values - jnp.einsum('smk,smr->skr', rigid_body_modes, scatter_copies, precision=HIGH_ACCURACY)

def dual_apply(entry_values, schur_blocks, pairing, signs):
    subs, width, columns = entry_values.shape
    shaped = entry_values.reshape(subs, NF, FS, columns)
    joined = signs * (shaped + partner_of(shaped, pairing))
    image = jnp.einsum('sij,sjr->sir', schur_blocks, joined.reshape(subs, width, columns), precision=HIGH_ACCURACY)
    signed = signs * image.reshape(subs, NF, FS, columns)
    return (signed + partner_of(signed, pairing)).reshape(subs, width, columns)

def reference(schur_blocks, rigid_body_modes, load_cases, face_sizes, contact_mask, friction_mask, cluster_ids, pairing):
    subs = schur_blocks.shape[0]
    positions = jnp.arange(FS, dtype=jnp.int32)
    inside = (positions[None, None, :] < face_sizes[:, :, None]).astype(jnp.float32).reshape(subs, NF * FS)
    blocked = (contact_mask * (1 - friction_mask)).astype(jnp.float32)
    free_mask = (inside * (1.0 - blocked))[:, :, None]
    choice_matrix = (cluster_ids[:, None] == jnp.arange(CLUSTERS, dtype=jnp.int32)[None, :]).astype(jnp.float32)
    local_gram = jnp.einsum('smk,snk->smn', rigid_body_modes, rigid_body_modes, precision=HIGH_ACCURACY)
    coarse_gram = jnp.einsum('sb,smn->bmn', choice_matrix, local_gram, precision=HIGH_ACCURACY)
    inverse = coarse_inverse(coarse_gram)
    signs = (1 - 2 * (jnp.arange(NF, dtype=jnp.int32) % 2)).astype(jnp.float32).reshape(1, NF, 1, 1)

    def operator(entry_values):
        projected = project(free_mask * entry_values, rigid_body_modes, choice_matrix, inverse)
        folded = dual_apply(projected, schur_blocks, pairing, signs)
        return free_mask * project(folded, rigid_body_modes, choice_matrix, inverse)
    residual = free_mask * project(free_mask * load_cases, rigid_body_modes, choice_matrix, inverse)
    direction = residual
    norm_now = jnp.sum(residual * residual, axis=(0, 1))
    multipliers = jnp.zeros_like(load_cases)
    for iteration in range(ITERS):
        image = operator(direction)
        step_size = norm_now / jnp.sum(direction * image, axis=(0, 1))
        multipliers = multipliers + step_size * direction
        residual = residual - step_size * image
        if iteration + 1 < ITERS:
            norm_next = jnp.sum(residual * residual, axis=(0, 1))
            direction = residual + norm_next / norm_now * direction
            norm_now = norm_next
    return (multipliers, residual)
```

```python
import functools

import jax
import jax.numpy as jnp
from jax import lax
from jax.experimental import pallas as pl
from jax.experimental.pallas import tpu as pltpu
from jax.sharding import PartitionSpec as P

MESH = pl.DeviceIdType.MESH
F32 = jnp.float32
BF16 = jnp.bfloat16
HIGHEST = lax.Precision.HIGHEST


def stage_plan(devices):
    plan = [(1, 2)]
    stride = 2
    while stride < devices:
        left = devices // stride
        radix = next(r for r in (4, 2, 3, 5, 7, left) if left % r == 0)
        plan.append((stride, radix))
        stride *= radix
    return plan


def kernel(
    subs,
    clusters,
    plan,
    schur_hbm,
    modes_ref,
    loads_ref,
    sizes_ref,
    contact_ref,
    friction_ref,
    cluster_ref,
    mult_ref,
    res_ref,
    s_buf,
    s_hi,
    s_lo,
    pack,
    pack_p,
    x_own,
    x_p,
    u_own,
    u_other,
    t_own,
    t_p,
    stacked,
    q_t,
    fr_t,
    mask_own,
    mask_sum,
    res0,
    res1,
    s_sem,
    ring_send,
    ring_recv,
    core_send,
    core_recv,
    red_send,
    red_recv,
    *slots,
):
    rows = loads_ref.shape[1]
    half = rows // 2
    cols = loads_ref.shape[2]
    n8 = 8 * clusters
    sub = lax.axis_index("sub")
    face = lax.axis_index("face")
    right = lax.rem(sub + 1, subs)
    left = lax.rem(sub + subs - 1, subs)
    linear = sub * 2 + face
    other = 1 - face

    peers = []
    for stride, radix in plan:
        digit = lax.rem(linear // stride, radix)
        group = []
        for k in range(1, radix):
            peer = linear + (lax.rem(digit + k, radix) - digit) * stride
            group.append((peer // 2, lax.rem(peer, 2)))
        peers.append((digit, group))

    barrier = pltpu.get_barrier_semaphore()
    total = 0
    for _, group in peers:
        for device in group:
            pl.semaphore_signal(barrier, inc=1, device_id=device, device_id_type=MESH)
            total += 1
    for device in ((right, face), (left, face)):
        pl.semaphore_signal(barrier, inc=1, device_id=device, device_id_type=MESH)
        total += 1

    other_cols = pl.multiple_of(other * rows, 128)
    own_cols = pl.multiple_of(face * rows, 128)
    s_copies = [
        pltpu.make_async_copy(schur_hbm.at[0, :, pl.ds(own_cols, rows)], s_buf.at[0], s_sem.at[0]),
        pltpu.make_async_copy(schur_hbm.at[0, :, pl.ds(other_cols, rows)], s_buf.at[1], s_sem.at[1]),
    ]
    for copy in s_copies:
        copy.start()

    sends = []

    def dot(a, b):
        return jnp.dot(a, b, preferred_element_type=F32, precision=HIGHEST)

    def ring(kind, src, dst, lanes):
        started = []
        for k, (device, lo, to) in enumerate(((right, 0, half), (left, half, 0))):
            if lanes:
                s_ref, d_ref = src.at[:, pl.ds(lo, half)], dst.at[:, pl.ds(to, half)]
            else:
                s_ref, d_ref = src.at[pl.ds(lo, half)], dst.at[pl.ds(to, half)]
            copy = pltpu.make_async_remote_copy(
                src_ref=s_ref,
                dst_ref=d_ref,
                send_sem=ring_send.at[2 * kind + k],
                recv_sem=ring_recv.at[2 * kind + k],
                device_id=(device, face),
                device_id_type=MESH,
            )
            copy.start()
            sends.append(copy)
            started.append(copy)
        return started

    def swap(index):
        copy = pltpu.make_async_remote_copy(
            src_ref=u_own.at[index],
            dst_ref=u_other.at[index],
            send_sem=core_send.at[index],
            recv_sem=core_recv.at[index],
            device_id=(sub, other),
            device_id_type=MESH,
        )
        copy.start()
        sends.append(copy)
        return copy

    per_red = sum(radix - 1 for _, radix in plan)

    def reduce_start(index, stage, store):
        ref = slots[index * len(plan) + stage]
        digit, group = peers[stage]
        store(ref, digit)
        base = index * per_red + sum(radix - 1 for _, radix in plan[:stage])
        copies = []
        for k, device in enumerate(group):
            copy = pltpu.make_async_remote_copy(
                src_ref=ref.at[digit],
                dst_ref=ref.at[digit],
                send_sem=red_send.at[base + k],
                recv_sem=red_recv.at[base + k],
                device_id=device,
                device_id_type=MESH,
            )
            copy.start()
            copies.append(copy)
            sends.append(copy)
        return ref, copies

    def reduce_end(started):
        ref, copies = started
        for copy in copies:
            copy.wait_recv()
        value = ref[0]
        for k in range(1, ref.shape[0]):
            value = value + ref[k]
        return value

    def put(value):
        def store(ref, digit):
            ref[digit] = value

        return store

    def all_reduce(index, store, meanwhile):
        started = reduce_start(index, 0, store)
        for stage in range(1, len(plan)):
            started = reduce_start(index, stage, put(reduce_end(started)))
        meanwhile()
        return reduce_end(started)

    position = lax.broadcasted_iota(jnp.int32, (1, half), 1)
    inside = jnp.concatenate(
        [
            jnp.where(position < sizes_ref[0, 0], 1.0, 0.0),
            jnp.where(position < sizes_ref[0, 1], 1.0, 0.0),
        ],
        axis=1,
    )
    blocked = (contact_ref[...] * (1 - friction_ref[...])).astype(F32)
    free = inside * (1.0 - blocked)
    pack[0:6, :] = modes_ref[0]
    pack[6:7, :] = jnp.full((1, rows), cluster_ref[0], jnp.int32).astype(F32)
    pack[7:8, :] = free

    def expand(ref):
        value = ref[...]
        row = lax.broadcasted_iota(jnp.int32, value.shape, 0)
        modes = jnp.where(row < 6, value, 0.0)
        ids = value[6:7, :]
        mask = value[7:8, :]
        per_cluster = jnp.concatenate(
            [jnp.where(ids == float(b), modes, 0.0) for b in range(clusters)], axis=0
        )
        return modes, per_cluster, per_cluster * mask, mask

    modes, rc, frc, mask = expand(pack)
    mask_own[...] = jnp.broadcast_to(mask, (128, rows)).T
    x_own[...] = loads_ref[0] * mask_own[...]
    stacked[...] = jnp.zeros_like(stacked)
    stacked[0:8, :] = modes
    stacked[8:16, :] = modes * mask
    gram_part = lax.dot_general(
        rc, stacked[...], (((1,), (1,)), ((), ())), preferred_element_type=F32, precision=HIGHEST
    )
    coarse_part = dot(rc, x_own[...])

    pl.semaphore_wait(barrier, total)

    def first_store(ref, digit):
        ref[digit, 0:n8, :] = coarse_part
        ref[digit, n8 : 2 * n8, :] = gram_part

    q = []

    def prepare():
        for k in range(2):
            s_copies[k].wait()
            value = s_buf[k]
            high = value.astype(BF16)
            s_hi[k] = high
            s_lo[k] = (value - high.astype(F32)).astype(BF16)
        for copy in pack_copies:
            copy.wait_recv()
        _, rc_p, frc_p, mask_p = expand(pack_p)
        both = jnp.concatenate([frc + frc_p, rc + rc_p], axis=0)
        q.append(both)
        q_t[...] = both.T
        fr_t[...] = frc.T
        mask_sum[...] = jnp.broadcast_to(mask + mask_p, (128, rows)).T
        for copy in x_copies:
            copy.wait_recv()

    started = reduce_start(0, 0, first_store)
    pack_copies = ring(0, pack, pack_p, True)
    x_copies = ring(1, x_own, x_p, False)
    for stage in range(1, len(plan)):
        started = reduce_start(0, stage, put(reduce_end(started)))
    prepare()
    first = reduce_end(started)
    q = q[0]

    shape3 = (clusters, 8, cols)
    coarse0 = first[0:n8].reshape(shape3)
    grams = first[n8 : 2 * n8].reshape(shape3)
    lane = lax.broadcasted_iota(jnp.int32, shape3, 2)
    row3 = lax.broadcasted_iota(jnp.int32, shape3, 1)
    work = (
        jnp.where(lane < 8, grams, 0.0)
        + jnp.where((lane == row3) & (row3 >= 6), 1.0, 0.0)
        + jnp.where(lane == row3 + 16, 1.0, 0.0)
    )
    for k in range(6):
        pivot_row = work[:, k : k + 1, :]
        pivot_row = pivot_row / pivot_row[:, :, k : k + 1]
        work = jnp.where(row3 == k, pivot_row, work - work[:, :, k : k + 1] * pivot_row)
    inv_cols = [jnp.broadcast_to(work[:, :, 16 + m : 17 + m], shape3) for m in range(6)]
    gf_cols = [jnp.broadcast_to(grams[:, :, 8 + m : 9 + m], shape3) for m in range(6)]

    def apply(columns, value):
        result = columns[0] * value[:, 0:1, :]
        for m in range(1, 6):
            result = result + columns[m] * value[:, m : m + 1, :]
        return result

    def flat(value):
        return value.reshape(n8, cols)

    def multiply(index, values):
        u_own[index, 0:half] = values[0:half]
        u_own[index, half:rows] = -values[half:rows]
        copy = swap(index)

        def part(k, value):
            high = value.astype(BF16)
            low = (value - high.astype(F32)).astype(BF16)
            wide = jnp.dot(
                s_hi[k], jnp.concatenate([high, low], axis=1), preferred_element_type=F32
            )
            narrow = jnp.dot(s_lo[k], high, preferred_element_type=F32)
            return wide[:, :cols] + wide[:, cols:] + narrow

        own = part(0, u_own[index])
        copy.wait_recv()
        image = own + part(1, u_other[index])
        t_own[index, 0:half] = image[0:half]
        t_own[index, half:rows] = -image[half:rows]

    def folded(index):
        return t_own[index] + t_p[index]

    def signed_u(index):
        return jnp.concatenate([u_own[index, 0:half], -u_own[index, half:rows]], axis=0)

    def sum_rows(value):
        return jnp.sum(value, axis=0, keepdims=True)

    c0 = apply(inv_cols, coarse0)
    coarse1 = coarse0 - apply(gf_cols, c0)
    w1 = apply(inv_cols, coarse1)
    x_both = x_own[...] + x_p[...]
    multiply(0, x_both - dot(q_t[...], jnp.concatenate([flat(c0), flat(w1)], axis=0)))
    t0_copies = ring(2, t_own.at[0], t_p.at[0], False)
    res0[...] = x_own[...] - dot(fr_t[...], flat(c0))

    def second_store(ref, digit):
        ref[digit, 0 : 2 * n8, :] = dot(q, t_own[0])
        ref[digit, 2 * n8 : 2 * n8 + 8, :] = jnp.zeros((8, cols), F32)
        ref[digit, 2 * n8 : 2 * n8 + 1, :] = sum_rows(signed_u(0) * t_own[0])
        ref[digit, 2 * n8 + 1 : 2 * n8 + 2, :] = sum_rows(res0[...] * res0[...])

    def wait_t0():
        for copy in t0_copies:
            copy.wait_recv()

    second = all_reduce(1, second_store, wait_t0)
    f_coarse = second[0:n8].reshape(shape3)
    r_coarse = second[n8 : 2 * n8].reshape(shape3)
    curvature0 = second[2 * n8 : 2 * n8 + 1]
    norm0 = second[2 * n8 + 1 : 2 * n8 + 2]
    step0 = norm0 / curvature0
    step_w = apply(inv_cols, r_coarse) * step0[None]
    coarse2 = coarse1 - step0[None] * f_coarse + apply(gf_cols, step_w)
    w2 = apply(inv_cols, coarse2)

    multiply(
        1,
        x_own[...]
        + x_p[...]
        - step0 * (mask_sum[...] * folded(0))
        - dot(q_t[...], jnp.concatenate([flat(c0 - step_w), flat(w2)], axis=0)),
    )
    t1_copies = ring(3, t_own.at[1], t_p.at[1], False)
    res1[...] = res0[...] - step0 * (mask_own[...] * folded(0)) + dot(fr_t[...], flat(step_w))

    def third_store(ref, digit):
        ref[digit, 0:n8, :] = dot(q[n8 : 2 * n8], t_own[1])
        ref[digit, n8 : n8 + 8, :] = jnp.zeros((8, cols), F32)
        ref[digit, n8 : n8 + 1, :] = sum_rows(signed_u(1) * t_own[1])
        ref[digit, n8 + 1 : n8 + 2, :] = sum_rows(signed_u(1) * t_own[0])
        ref[digit, n8 + 2 : n8 + 3, :] = sum_rows(res1[...] * res1[...])

    def wait_t1():
        for copy in t1_copies:
            copy.wait_recv()

    third = all_reduce(2, third_store, wait_t1)
    norm1 = third[n8 + 2 : n8 + 3]
    ratio = norm1 / norm0
    curvature1 = (
        third[n8 : n8 + 1] + ratio * (2.0 * third[n8 + 1 : n8 + 2]) + ratio * (ratio * curvature0)
    )
    step1 = norm1 / curvature1
    w_out = apply(inv_cols, third[0:n8].reshape(shape3) + ratio[None] * r_coarse) * step1[None]
    mult_ref[0] = step0 * res0[...] + step1 * (res1[...] + ratio * res0[...])
    res_ref[0] = (
        res1[...]
        - step1 * (mask_own[...] * (folded(1) + ratio * folded(0)))
        + dot(fr_t[...], flat(w_out))
    )
    for copy in sends:
        copy.wait_send()


def solution(mesh):
    subs = mesh.shape["sub"]
    devices = subs * mesh.shape["face"]
    plan = stage_plan(devices)

    def on_device(schur, modes, loads, sizes, contact, friction, cluster_ids, pairing):
        del pairing
        _, rows, cols = loads.shape
        clusters = subs // 8
        n8 = 8 * clusters
        vmem = pl.BlockSpec(memory_space=pltpu.VMEM)
        smem = pl.BlockSpec(memory_space=pltpu.SMEM)
        field = pltpu.VMEM((rows, cols), F32)
        pair = pltpu.VMEM((2, rows, cols), F32)
        slot_rows = (2 * n8, 2 * n8 + 8, n8 + 8)
        slots = [pltpu.VMEM((radix, count, cols), F32) for count in slot_rows for _, radix in plan]
        reds = 3 * sum(radix - 1 for _, radix in plan)
        return pl.pallas_call(
            functools.partial(kernel, subs, clusters, plan),
            out_shape=[jax.ShapeDtypeStruct(loads.shape, F32)] * 2,
            in_specs=[pl.BlockSpec(memory_space=pl.ANY), vmem, vmem, smem, vmem, vmem, smem],
            out_specs=[vmem, vmem],
            scratch_shapes=[
                pltpu.VMEM((2, rows, rows), F32),
                pltpu.VMEM((2, rows, rows), BF16),
                pltpu.VMEM((2, rows, rows), BF16),
                pltpu.VMEM((8, rows), F32),
                pltpu.VMEM((8, rows), F32),
                field,
                field,
                pair,
                pair,
                pair,
                pair,
                pltpu.VMEM((128, rows), F32),
                pltpu.VMEM((rows, 2 * n8), F32),
                pltpu.VMEM((rows, n8), F32),
                field,
                field,
                field,
                field,
                pltpu.SemaphoreType.DMA((2,)),
                pltpu.SemaphoreType.DMA((8,)),
                pltpu.SemaphoreType.DMA((8,)),
                pltpu.SemaphoreType.DMA((2,)),
                pltpu.SemaphoreType.DMA((2,)),
                pltpu.SemaphoreType.DMA((reds,)),
                pltpu.SemaphoreType.DMA((reds,)),
                *slots,
            ],
            compiler_params=pltpu.CompilerParams(
                collective_id=0, has_side_effects=True, vmem_limit_bytes=48 * 1024 * 1024
            ),
        )(schur, modes, loads, sizes, contact, friction, cluster_ids)

    placed = (
        P("sub", "face", None),
        P("sub", None, "face"),
        P("sub", "face", None),
        P("sub", "face"),
        P("sub", "face"),
        P("sub", "face"),
        P("sub"),
        P("sub", "face", None, None),
    )
    return jax.shard_map(
        on_device,
        mesh=mesh,
        in_specs=placed,
        out_specs=(P("sub", "face", None), P("sub", "face", None)),
        check_vma=False,
    )
```

```python
import functools

import jax
import jax.numpy as jnp
from jax import lax
from jax.experimental import pallas as pl
from jax.experimental.pallas import tpu as pltpu
from jax.sharding import PartitionSpec as P

MESH = pl.DeviceIdType.MESH
F32 = jnp.float32
BF16 = jnp.bfloat16
HIGHEST = lax.Precision.HIGHEST


def stage_plan(devices):
    plan = []
    stride = 2
    while stride < devices:
        left = devices // stride
        radix = next(r for r in (4, 2, 3, 5, 7, left) if left % r == 0)
        plan.append((stride, radix))
        stride *= radix
    return [(1, 2)] + plan[::-1]


def kernel(
    subs,
    clusters,
    plan,
    schur_hbm,
    modes_hbm,
    loads_hbm,
    sizes_hbm,
    contact_hbm,
    friction_hbm,
    cluster_hbm,
    mult_ref,
    res_ref,
    s_buf,
    loads_buf,
    modes_buf,
    contact_buf,
    friction_buf,
    sizes_buf,
    cluster_buf,
    s_hi,
    s_lo,
    pack,
    pack_p,
    q_own,
    q_other,
    x_own,
    x_p,
    v_own,
    v_other,
    y_own,
    y_p,
    stacked,
    low_image,
    low_u,
    low_res,
    mask_own,
    mask_sum,
    image,
    u_now,
    res0,
    res1,
    in_sem,
    ring_send,
    ring_recv,
    core_send,
    core_recv,
    red_send,
    red_recv,
    *slots,
):
    rows, cols = loads_buf.shape
    half = rows // 2
    n8 = 8 * clusters
    sub = lax.axis_index("sub")
    face = lax.axis_index("face")
    right = lax.rem(sub + 1, subs)
    left = lax.rem(sub + subs - 1, subs)
    linear = sub * 2 + face
    other = 1 - face

    own_cols = pl.multiple_of(face * rows, 128)
    other_cols = pl.multiple_of(other * rows, 128)
    inputs = [
        pltpu.make_async_copy(src, dst, in_sem.at[k])
        for k, (src, dst) in enumerate(
            (
                (sizes_hbm, sizes_buf),
                (cluster_hbm, cluster_buf),
                (contact_hbm, contact_buf),
                (friction_hbm, friction_buf),
                (modes_hbm, modes_buf),
                (loads_hbm.at[0], loads_buf),
                (schur_hbm.at[0, :, pl.ds(own_cols, rows)], s_buf.at[0]),
                (schur_hbm.at[0, :, pl.ds(other_cols, rows)], s_buf.at[1]),
            )
        )
    ]
    for copy in inputs:
        copy.start()

    peers = []
    for stride, radix in plan:
        digit = lax.rem(linear // stride, radix)
        group = []
        for k in range(1, radix):
            peer = linear + (lax.rem(digit + k, radix) - digit) * stride
            group.append((peer // 2, lax.rem(peer, 2)))
        peers.append((digit, group))

    barrier = pltpu.get_barrier_semaphore()
    total = 0
    for _, group in peers:
        for device in group:
            pl.semaphore_signal(barrier, inc=1, device_id=device, device_id_type=MESH)
            total += 1
    for device in ((right, face), (left, face)):
        pl.semaphore_signal(barrier, inc=1, device_id=device, device_id_type=MESH)
        total += 1

    sends = []

    def dot(a, b):
        return jnp.dot(a, b, preferred_element_type=F32, precision=HIGHEST)

    def ring(kind, src, dst, lanes):
        started = []
        for k, (device, lo, to) in enumerate(((right, 0, half), (left, half, 0))):
            if lanes:
                s_ref, d_ref = src.at[:, pl.ds(lo, half)], dst.at[:, pl.ds(to, half)]
            else:
                s_ref, d_ref = src.at[pl.ds(lo, half)], dst.at[pl.ds(to, half)]
            copy = pltpu.make_async_remote_copy(
                src_ref=s_ref,
                dst_ref=d_ref,
                send_sem=ring_send.at[2 * kind + k],
                recv_sem=ring_recv.at[2 * kind + k],
                device_id=(device, face),
                device_id_type=MESH,
            )
            copy.start()
            sends.append(copy)
            started.append(copy)
        return started

    def swap(index, src, dst):
        copy = pltpu.make_async_remote_copy(
            src_ref=src,
            dst_ref=dst,
            send_sem=core_send.at[index],
            recv_sem=core_recv.at[index],
            device_id=(sub, other),
            device_id_type=MESH,
        )
        copy.start()
        sends.append(copy)
        return copy

    per_red = sum(radix - 1 for _, radix in plan)

    def reduce_start(index, stage, store):
        ref = slots[index * len(plan) + stage]
        digit, group = peers[stage]
        store(ref, digit)
        base = index * per_red + sum(radix - 1 for _, radix in plan[:stage])
        copies = []
        for k, device in enumerate(group):
            copy = pltpu.make_async_remote_copy(
                src_ref=ref.at[digit],
                dst_ref=ref.at[digit],
                send_sem=red_send.at[base + k],
                recv_sem=red_recv.at[base + k],
                device_id=device,
                device_id_type=MESH,
            )
            copy.start()
            copies.append(copy)
            sends.append(copy)
        return ref, copies

    def reduce_end(started):
        ref, copies = started
        for copy in copies:
            copy.wait_recv()
        value = ref[0]
        for k in range(1, ref.shape[0]):
            value = value + ref[k]
        return value

    def put(value):
        def store(ref, digit):
            ref[digit] = value

        return store

    def all_reduce(index, store, meanwhile):
        started = reduce_start(index, 0, store)
        for stage in range(1, len(plan)):
            if stage - 1 < len(meanwhile) - 1:
                meanwhile[stage - 1]()
            started = reduce_start(index, stage, put(reduce_end(started)))
        meanwhile[-1]()
        return reduce_end(started)

    def split3(value):
        first = value.astype(BF16)
        rest = value - first.astype(F32)
        second = rest.astype(BF16)
        third = (rest - second.astype(F32)).astype(BF16)
        return first, second, third

    def low_left(value):
        a, b, c = split3(value)
        return jnp.concatenate([a, a, a, b, b, c], axis=1)

    def low_right(value):
        a, b, c = split3(value)
        return jnp.concatenate([a, b, c, a, b, a], axis=0)

    def bdot(a, b):
        return jnp.dot(a, b, preferred_element_type=F32)

    for copy in inputs[:5]:
        copy.wait()
    position = lax.broadcasted_iota(jnp.int32, (1, half), 1)
    inside = jnp.concatenate(
        [
            jnp.where(position < sizes_buf[0, 0], 1.0, 0.0),
            jnp.where(position < sizes_buf[0, 1], 1.0, 0.0),
        ],
        axis=1,
    )
    blocked = (contact_buf[...] * (1 - friction_buf[...])).astype(F32)
    free = inside * (1.0 - blocked)
    for m in range(6):
        pack[m : m + 1, :] = modes_buf[m]
    pack[6:7, :] = jnp.full((1, rows), cluster_buf[0], jnp.int32).astype(F32)
    pack[7:8, :] = free

    def expand(ref):
        value = ref[...]
        row = lax.broadcasted_iota(jnp.int32, value.shape, 0)
        modes = jnp.where(row < 6, value, 0.0)
        ids = value[6:7, :]
        mask = value[7:8, :]
        per_cluster = jnp.concatenate(
            [jnp.where(ids == float(b), modes, 0.0) for b in range(clusters)], axis=0
        )
        return modes, per_cluster, per_cluster * mask, mask

    modes, rc, frc, mask = expand(pack)
    lane_sign = jnp.where(lax.broadcasted_iota(jnp.int32, (1, rows), 1) < half, 1.0, -1.0)
    mask_wide = jnp.broadcast_to(mask, (128, rows)).T
    inputs[5].wait()
    x_own[...] = loads_buf[...] * mask_wide
    pl.semaphore_wait(barrier, total)
    pack_copies = ring(0, pack, pack_p, True)
    x_copies = ring(1, x_own, x_p, False)

    stacked[...] = jnp.zeros_like(stacked)
    stacked[0:8, :] = modes
    stacked[8:16, :] = modes * mask

    def first_store(ref, digit):
        ref[digit, 0:n8, :] = dot(rc, x_own[...])
        ref[digit, n8 : 2 * n8, :] = lax.dot_general(
            rc, stacked[...], (((1,), (1,)), ((), ())), preferred_element_type=F32, precision=HIGHEST
        )

    def split_schur():
        mask_own[0:half] = mask_wide[0:half]
        mask_own[half:rows] = -mask_wide[half:rows]
        for k in range(2):
            inputs[6 + k].wait()
            value = s_buf[k]
            high = value.astype(BF16)
            s_hi[k, 0:rows] = high
            s_lo[k, 0:rows] = (value - high.astype(F32)).astype(BF16)

    def product(value_own, fetch_other):
        def part(k, value):
            high = value.astype(BF16)
            low = (value - high.astype(F32)).astype(BF16)
            wide = bdot(s_hi[k], jnp.concatenate([high, low], axis=1))
            return wide[:, :cols] + wide[:, cols:] + bdot(s_lo[k], high)

        own = part(0, value_own)
        return own + part(1, fetch_other())

    swapped = []

    def fold_modes():
        for copy in pack_copies:
            copy.wait_recv()
        _, rc_p, frc_p, mask_p = expand(pack_p)
        q_own[...] = jnp.concatenate([frc + frc_p, rc + rc_p], axis=0) * lane_sign
        swapped.append(swap(0, q_own, q_other))
        mask_sum[...] = jnp.broadcast_to(mask + mask_p, (128, rows)).T
        split_schur()

    def swap_product(index):
        copy = swap(1 + index, v_own.at[index], v_other.at[index])

        def fetch():
            copy.wait_recv()
            return v_other[index]

        return product(v_own[index], fetch)

    def first_product():
        q = q_own[...]
        q_high = q.astype(BF16)
        q_low = (q - q_high.astype(F32)).astype(BF16)
        for k in range(2):
            wide = bdot(jnp.concatenate([q_high, q_low], axis=0), s_hi[k, 0:rows])
            coarse = wide[0 : 2 * n8] + wide[2 * n8 :] + bdot(q_high, s_lo[k, 0:rows])
            high = coarse.astype(BF16)
            s_hi[k, rows : rows + 2 * n8] = high
            s_lo[k, rows : rows + 2 * n8] = (coarse - high.astype(F32)).astype(BF16)
        q_t = q.T
        low_u[...] = low_left(q_t)
        low_res[...] = low_left(
            jnp.concatenate([frc.T, jnp.zeros((rows, n8), F32)], axis=1)
        )
        swapped[0].wait_recv()
        total_image = jnp.zeros((rows + 2 * n8, 2 * n8), F32)
        for k, value in enumerate((q_t, q_other[...].T)):
            high = value.astype(BF16)
            low = (value - high.astype(F32)).astype(BF16)
            total_image += bdot(s_hi[k], high) + bdot(s_hi[k], low) + bdot(s_lo[k], high)
        low_image[...] = low_left(total_image)
        for copy in x_copies:
            copy.wait_recv()
        both = x_own[...] + x_p[...]
        v_own[0, 0:half] = both[0:half]
        v_own[0, half:rows] = -both[half:rows]
        image[...] = swap_product(0)

    first = all_reduce(0, first_store, [fold_modes, first_product])

    shape3 = (clusters, 8, cols)
    coarse0 = first[0:n8].reshape(shape3)
    grams = first[n8 : 2 * n8].reshape(shape3)
    lane = lax.broadcasted_iota(jnp.int32, shape3, 2)
    row3 = lax.broadcasted_iota(jnp.int32, shape3, 1)
    work = (
        jnp.where(lane < 8, grams, 0.0)
        + jnp.where((lane == row3) & (row3 >= 6), 1.0, 0.0)
        + jnp.where(lane == row3 + 16, 1.0, 0.0)
    )
    for k in range(6):
        pivot_row = work[:, k : k + 1, :]
        pivot_row = pivot_row / pivot_row[:, :, k : k + 1]
        work = jnp.where(row3 == k, pivot_row, work - work[:, :, k : k + 1] * pivot_row)
    inv_cols = [jnp.broadcast_to(work[:, :, 16 + m : 17 + m], shape3) for m in range(6)]
    gf_cols = [jnp.broadcast_to(grams[:, :, 8 + m : 9 + m], shape3) for m in range(6)]

    def apply(columns, value):
        result = columns[0] * value[:, 0:1, :]
        for m in range(1, 6):
            result = result + columns[m] * value[:, m : m + 1, :]
        return result

    def flat(value):
        return value.reshape(n8, cols)

    def pair(a, b):
        return low_right(jnp.concatenate([flat(a), flat(b)], axis=0))

    def sum_rows(value):
        return jnp.sum(value, axis=0, keepdims=True)

    c0 = apply(inv_cols, coarse0)
    coarse1 = coarse0 - apply(gf_cols, c0)
    w1 = apply(inv_cols, coarse1)
    weights0 = pair(c0, w1)
    now = image[...] - bdot(low_image[...], weights0)
    y_own[0] = now[0:rows]
    y0_copies = ring(2, y_own.at[0], y_p.at[0], False)
    coarse_rows0 = now[rows:]
    image[rows:] = coarse_rows0

    def second_store(ref, digit):
        u_now[...] = v_own[0] - bdot(low_u[...], weights0)
        res0[...] = x_own[...] - bdot(low_res[...], weights0)
        ref[digit, 0 : 2 * n8, :] = coarse_rows0
        ref[digit, 2 * n8 : 2 * n8 + 8, :] = jnp.zeros((8, cols), F32)
        ref[digit, 2 * n8 : 2 * n8 + 1, :] = sum_rows(u_now[...] * y_own[0])
        ref[digit, 2 * n8 + 1 : 2 * n8 + 2, :] = sum_rows(res0[...] * res0[...])

    second_image = []

    def second_product():
        for copy in y0_copies:
            copy.wait_recv()
        v_own[1] = mask_sum[...] * (y_own[0] - y_p[0])
        second_image.append(swap_product(1))

    second = all_reduce(1, second_store, [second_product])
    f_coarse = second[0:n8].reshape(shape3)
    r_coarse = second[n8 : 2 * n8].reshape(shape3)
    curvature0 = second[2 * n8 : 2 * n8 + 1]
    norm0 = second[2 * n8 + 1 : 2 * n8 + 2]
    step0 = norm0 / curvature0
    step_w = apply(inv_cols, r_coarse) * step0[None]
    coarse2 = coarse1 - step0[None] * f_coarse + apply(gf_cols, step_w)
    w2 = apply(inv_cols, coarse2)

    weights1 = pair(step_w, w1 - w2)
    change = second_image[0] * step0 - bdot(low_image[...], weights1)
    y_own[1] = y_own[0] - change[0:rows]
    y1_copies = ring(3, y_own.at[1], y_p.at[1], False)

    def third_store(ref, digit):
        u_next = u_now[...] - step0 * v_own[1] + bdot(low_u[...], weights1)
        res1[...] = (
            res0[...]
            - step0 * (mask_own[...] * (y_own[0] - y_p[0]))
            + bdot(low_res[...], weights1)
        )
        ref[digit, 0:n8, :] = image[rows + n8 :] - change[rows + n8 :]
        ref[digit, n8 : n8 + 8, :] = jnp.zeros((8, cols), F32)
        ref[digit, n8 : n8 + 1, :] = sum_rows(u_next * y_own[1])
        ref[digit, n8 + 1 : n8 + 2, :] = sum_rows(u_next * y_own[0])
        ref[digit, n8 + 2 : n8 + 3, :] = sum_rows(res1[...] * res1[...])

    def wait_y1():
        for copy in y1_copies:
            copy.wait_recv()

    third = all_reduce(2, third_store, [wait_y1])
    norm1 = third[n8 + 2 : n8 + 3]
    ratio = norm1 / norm0
    curvature1 = (
        third[n8 : n8 + 1] + ratio * (2.0 * third[n8 + 1 : n8 + 2]) + ratio * (ratio * curvature0)
    )
    step1 = norm1 / curvature1
    w_out = apply(inv_cols, third[0:n8].reshape(shape3) + ratio[None] * r_coarse) * step1[None]
    mult_ref[0] = step0 * res0[...] + step1 * (res1[...] + ratio * res0[...])
    jump = (y_own[1] - y_p[1]) + ratio * (y_own[0] - y_p[0])
    res_ref[0] = (
        res1[...]
        - step1 * (mask_own[...] * jump)
        + bdot(low_res[...], pair(w_out, jnp.zeros_like(w_out)))
    )
    for copy in sends:
        copy.wait_send()


def solution(mesh):
    subs = mesh.shape["sub"]
    devices = subs * mesh.shape["face"]
    plan = stage_plan(devices)

    def on_device(schur, modes, loads, sizes, contact, friction, cluster_ids, pairing):
        del pairing
        _, rows, cols = loads.shape
        clusters = subs // 8
        n8 = 8 * clusters
        vmem = pl.BlockSpec(memory_space=pltpu.VMEM)
        field = pltpu.VMEM((rows, cols), F32)
        pair = pltpu.VMEM((2, rows, cols), F32)
        slot_rows = (2 * n8, 2 * n8 + 8, n8 + 8)
        slots = [pltpu.VMEM((radix, count, cols), F32) for count in slot_rows for _, radix in plan]
        reds = 3 * sum(radix - 1 for _, radix in plan)
        anywhere = pl.BlockSpec(memory_space=pl.ANY)
        tall = rows + 2 * n8
        return pl.pallas_call(
            functools.partial(kernel, subs, clusters, plan),
            out_shape=[jax.ShapeDtypeStruct(loads.shape, F32)] * 2,
            in_specs=[anywhere] * 7,
            out_specs=[vmem, vmem],
            scratch_shapes=[
                pltpu.VMEM((2, rows, rows), F32),
                field,
                pltpu.VMEM((6, 1, rows), F32),
                pltpu.VMEM((1, rows), jnp.int32),
                pltpu.VMEM((1, rows), jnp.int32),
                pltpu.SMEM((1, 2), jnp.int32),
                pltpu.SMEM((1,), jnp.int32),
                pltpu.VMEM((2, tall, rows), BF16),
                pltpu.VMEM((2, tall, rows), BF16),
                pltpu.VMEM((8, rows), F32),
                pltpu.VMEM((8, rows), F32),
                pltpu.VMEM((2 * n8, rows), F32),
                pltpu.VMEM((2 * n8, rows), F32),
                field,
                field,
                pair,
                pair,
                pair,
                pair,
                pltpu.VMEM((128, rows), F32),
                pltpu.VMEM((tall, 12 * n8), BF16),
                pltpu.VMEM((rows, 12 * n8), BF16),
                pltpu.VMEM((rows, 12 * n8), BF16),
                field,
                field,
                pltpu.VMEM((tall, cols), F32),
                field,
                field,
                field,
                pltpu.SemaphoreType.DMA((8,)),
                pltpu.SemaphoreType.DMA((8,)),
                pltpu.SemaphoreType.DMA((8,)),
                pltpu.SemaphoreType.DMA((3,)),
                pltpu.SemaphoreType.DMA((3,)),
                pltpu.SemaphoreType.DMA((reds,)),
                pltpu.SemaphoreType.DMA((reds,)),
                *slots,
            ],
            compiler_params=pltpu.CompilerParams(
                collective_id=0, has_side_effects=True, vmem_limit_bytes=60 * 1024 * 1024
            ),
        )(
            schur,
            modes.reshape(modes.shape[1], 1, rows),
            loads,
            sizes,
            contact,
            friction,
            cluster_ids,
        )

    placed = (
        P("sub", "face", None),
        P("sub", None, "face"),
        P("sub", "face", None),
        P("sub", "face"),
        P("sub", "face"),
        P("sub", "face"),
        P("sub"),
        P("sub", "face", None, None),
    )
    return jax.shard_map(
        on_device,
        mesh=mesh,
        in_specs=placed,
        out_specs=(P("sub", "face", None), P("sub", "face", None)),
        check_vma=False,
    )
```

```python
import functools

import jax
import jax.numpy as jnp
from jax import lax
from jax.experimental import pallas as pl
from jax.experimental.pallas import tpu as pltpu
from jax.sharding import PartitionSpec as P

MESH = pl.DeviceIdType.MESH
F32 = jnp.float32
BF16 = jnp.bfloat16
HIGHEST = lax.Precision.HIGHEST


def stage_plan(devices):
    plan = []
    stride = 2
    while stride < devices:
        left = devices // stride
        radix = next(r for r in (4, 2, 3, 5, 7, left) if left % r == 0)
        plan.append((stride, radix))
        stride *= radix
    return plan[:0:-1] + [(1, 2 * plan[0][1])]


def kernel(
    subs,
    clusters,
    plan,
    schur_hbm,
    modes_hbm,
    loads_hbm,
    sizes_hbm,
    contact_hbm,
    friction_hbm,
    cluster_hbm,
    mult_ref,
    res_ref,
    s_buf,
    loads_buf,
    modes_buf,
    contact_buf,
    friction_buf,
    sizes_buf,
    cluster_buf,
    s_hi,
    s_lo,
    pack,
    pack_p,
    q_own,
    q_other,
    x_own,
    x_p,
    v_own,
    v_other,
    y_own,
    y_p,
    stacked,
    low_image,
    low_u,
    low_res,
    mask_own,
    mask_sum,
    image,
    u_now,
    res0,
    res1,
    in_sem,
    ring_send,
    ring_recv,
    core_send,
    core_recv,
    red_send,
    red_recv,
    *slots,
):
    rows, cols = loads_buf.shape
    half = rows // 2
    n8 = 8 * clusters
    sub = lax.axis_index("sub")
    face = lax.axis_index("face")
    right = lax.rem(sub + 1, subs)
    left = lax.rem(sub + subs - 1, subs)
    linear = sub * 2 + face
    other = 1 - face

    own_cols = pl.multiple_of(face * rows, 128)
    other_cols = pl.multiple_of(other * rows, 128)
    inputs = [
        pltpu.make_async_copy(src, dst, in_sem.at[k])
        for k, (src, dst) in enumerate(
            (
                (sizes_hbm, sizes_buf),
                (cluster_hbm, cluster_buf),
                (contact_hbm, contact_buf),
                (friction_hbm, friction_buf),
                (modes_hbm, modes_buf),
                (loads_hbm.at[0], loads_buf),
                (schur_hbm.at[0, :, pl.ds(own_cols, rows)], s_buf.at[0]),
                (schur_hbm.at[0, :, pl.ds(other_cols, rows)], s_buf.at[1]),
            )
        )
    ]
    for copy in inputs:
        copy.start()

    peers = []
    for stride, radix in plan:
        digit = lax.rem(linear // stride, radix)
        group = []
        for k in range(1, radix):
            peer = linear + (lax.rem(digit + k, radix) - digit) * stride
            group.append((peer // 2, lax.rem(peer, 2)))
        peers.append((digit, group))

    barrier = pltpu.get_barrier_semaphore()
    total = 0
    for _, group in peers:
        for device in group:
            pl.semaphore_signal(barrier, inc=1, device_id=device, device_id_type=MESH)
            total += 1
    for device in ((right, face), (left, face)):
        pl.semaphore_signal(barrier, inc=1, device_id=device, device_id_type=MESH)
        total += 1

    sends = []

    def dot(a, b):
        return jnp.dot(a, b, preferred_element_type=F32, precision=HIGHEST)

    def ring(kind, src, dst, lanes):
        started = []
        for k, (device, lo, to) in enumerate(((right, 0, half), (left, half, 0))):
            if lanes:
                s_ref, d_ref = src.at[:, pl.ds(lo, half)], dst.at[:, pl.ds(to, half)]
            else:
                s_ref, d_ref = src.at[pl.ds(lo, half)], dst.at[pl.ds(to, half)]
            copy = pltpu.make_async_remote_copy(
                src_ref=s_ref,
                dst_ref=d_ref,
                send_sem=ring_send.at[2 * kind + k],
                recv_sem=ring_recv.at[2 * kind + k],
                device_id=(device, face),
                device_id_type=MESH,
            )
            copy.start()
            sends.append(copy)
            started.append(copy)
        return started

    def swap(index, src, dst):
        copy = pltpu.make_async_remote_copy(
            src_ref=src,
            dst_ref=dst,
            send_sem=core_send.at[index],
            recv_sem=core_recv.at[index],
            device_id=(sub, other),
            device_id_type=MESH,
        )
        copy.start()
        sends.append(copy)
        return copy

    per_red = sum(radix - 1 for _, radix in plan)

    def reduce_start(index, stage, store):
        ref = slots[index * len(plan) + stage]
        digit, group = peers[stage]
        store(ref, digit)
        base = index * per_red + sum(radix - 1 for _, radix in plan[:stage])
        copies = []
        for k, device in enumerate(group):
            copy = pltpu.make_async_remote_copy(
                src_ref=ref.at[digit],
                dst_ref=ref.at[digit],
                send_sem=red_send.at[base + k],
                recv_sem=red_recv.at[base + k],
                device_id=device,
                device_id_type=MESH,
            )
            copy.start()
            copies.append(copy)
            sends.append(copy)
        return ref, copies

    def reduce_end(started):
        ref, copies = started
        for copy in copies:
            copy.wait_recv()
        value = ref[0]
        for k in range(1, ref.shape[0]):
            value = value + ref[k]
        return value

    def put(value):
        def store(ref, digit):
            ref[digit] = value

        return store

    def all_reduce(index, store, meanwhile):
        started = reduce_start(index, 0, store)
        for stage in range(1, len(plan)):
            if stage - 1 < len(meanwhile) - 1:
                meanwhile[stage - 1]()
            started = reduce_start(index, stage, put(reduce_end(started)))
        meanwhile[-1]()
        return reduce_end(started)

    def split3(value):
        first = value.astype(BF16)
        rest = value - first.astype(F32)
        second = rest.astype(BF16)
        third = (rest - second.astype(F32)).astype(BF16)
        return first, second, third

    def low_left(value):
        count = value.shape[1]
        row = lax.broadcasted_iota(jnp.int32, (count, 6 * count), 0)
        col = lax.broadcasted_iota(jnp.int32, (count, 6 * count), 1)
        total_spread = 0.0
        for piece, (lo, hi) in zip(split3(value), ((0, 3), (3, 5), (5, 6))):
            spread = jnp.zeros(row.shape, F32)
            for k in range(lo, hi):
                spread += jnp.where(col == row + k * count, 1.0, 0.0)
            total_spread += bdot(piece, spread.astype(BF16))
        return total_spread.astype(BF16)

    def low_right(value):
        a, b, c = split3(value)
        return jnp.concatenate([a, b, c, a, b, a], axis=0)

    def bdot(a, b):
        return jnp.dot(a, b, preferred_element_type=F32)

    for copy in inputs[:5]:
        copy.wait()
    position = lax.broadcasted_iota(jnp.int32, (1, half), 1)
    inside = jnp.concatenate(
        [
            jnp.where(position < sizes_buf[0, 0], 1.0, 0.0),
            jnp.where(position < sizes_buf[0, 1], 1.0, 0.0),
        ],
        axis=1,
    )
    blocked = (contact_buf[...] * (1 - friction_buf[...])).astype(F32)
    free = inside * (1.0 - blocked)
    for m in range(6):
        pack[m : m + 1, :] = modes_buf[m]
    pack[6:7, :] = jnp.full((1, rows), cluster_buf[0], jnp.int32).astype(F32)
    pack[7:8, :] = free

    def expand(ref):
        value = ref[...]
        row = lax.broadcasted_iota(jnp.int32, value.shape, 0)
        modes = jnp.where(row < 6, value, 0.0)
        ids = value[6:7, :]
        mask = value[7:8, :]
        per_cluster = jnp.concatenate(
            [jnp.where(ids == float(b), modes, 0.0) for b in range(clusters)], axis=0
        )
        return modes, per_cluster, per_cluster * mask, mask

    modes, rc, frc, mask = expand(pack)
    lane_sign = jnp.where(lax.broadcasted_iota(jnp.int32, (1, rows), 1) < half, 1.0, -1.0)
    mask_wide = jnp.broadcast_to(mask, (128, rows)).T
    inputs[5].wait()
    x_own[...] = loads_buf[...] * mask_wide
    pl.semaphore_wait(barrier, total)
    pack_copies = ring(0, pack, pack_p, True)
    x_copies = ring(1, x_own, x_p, False)

    stacked[...] = jnp.zeros_like(stacked)
    stacked[0:8, :] = modes
    stacked[8:16, :] = modes * mask

    def first_store(ref, digit):
        ref[digit, 0:n8, :] = dot(rc, x_own[...])
        ref[digit, n8 : 2 * n8, :] = lax.dot_general(
            rc, stacked[...], (((1,), (1,)), ((), ())), preferred_element_type=F32, precision=HIGHEST
        )

    def split_schur():
        mask_own[0:half] = mask_wide[0:half]
        mask_own[half:rows] = -mask_wide[half:rows]
        for k in range(2):
            inputs[6 + k].wait()
            value = s_buf[k]
            high = value.astype(BF16)
            s_hi[k, 0:rows] = high
            s_lo[k, 0:rows] = (value - high.astype(F32)).astype(BF16)

    def product(value_own, fetch_other):
        def part(k, value):
            high = value.astype(BF16)
            low = (value - high.astype(F32)).astype(BF16)
            wide = bdot(s_hi[k], jnp.concatenate([high, low], axis=1))
            return wide[:, :cols] + wide[:, cols:] + bdot(s_lo[k], high)

        own = part(0, value_own)
        return own + part(1, fetch_other())

    swapped = []

    def fold_modes():
        for copy in pack_copies:
            copy.wait_recv()
        _, rc_p, frc_p, mask_p = expand(pack_p)
        q_own[...] = jnp.concatenate([frc + frc_p, rc + rc_p], axis=0) * lane_sign
        swapped.append(swap(0, q_own, q_other))
        mask_sum[...] = jnp.broadcast_to(mask + mask_p, (128, rows)).T
        split_schur()

    def swap_product(index):
        copy = swap(1 + index, v_own.at[index], v_other.at[index])

        def fetch():
            copy.wait_recv()
            return v_other[index]

        return product(v_own[index], fetch)

    def first_product():
        q = q_own[...]
        q_high = q.astype(BF16)
        q_low = (q - q_high.astype(F32)).astype(BF16)
        for k in range(2):
            wide = bdot(jnp.concatenate([q_high, q_low], axis=0), s_hi[k, 0:rows])
            coarse = wide[0 : 2 * n8] + wide[2 * n8 :] + bdot(q_high, s_lo[k, 0:rows])
            high = coarse.astype(BF16)
            s_hi[k, rows : rows + 2 * n8] = high
            s_lo[k, rows : rows + 2 * n8] = (coarse - high.astype(F32)).astype(BF16)
        q_t = q.T
        low_u[...] = low_left(q_t)
        low_res[...] = low_left(
            jnp.concatenate([frc.T, jnp.zeros((rows, n8), F32)], axis=1)
        )
        swapped[0].wait_recv()
        total_image = jnp.zeros((rows + 2 * n8, 2 * n8), F32)
        for k, value in enumerate((q_t, q_other[...].T)):
            high = value.astype(BF16)
            low = (value - high.astype(F32)).astype(BF16)
            total_image += bdot(s_hi[k], high) + bdot(s_hi[k], low) + bdot(s_lo[k], high)
        low_image[...] = low_left(total_image)
        for copy in x_copies:
            copy.wait_recv()
        both = x_own[...] + x_p[...]
        v_own[0, 0:half] = both[0:half]
        v_own[0, half:rows] = -both[half:rows]
        image[...] = swap_product(0)

    first = all_reduce(0, first_store, [fold_modes, first_product])

    shape3 = (clusters, 8, cols)
    coarse0 = first[0:n8].reshape(shape3)
    grams = first[n8 : 2 * n8].reshape(shape3)
    lane = lax.broadcasted_iota(jnp.int32, shape3, 2)
    row3 = lax.broadcasted_iota(jnp.int32, shape3, 1)
    work = (
        jnp.where(lane < 8, grams, 0.0)
        + jnp.where((lane == row3) & (row3 >= 6), 1.0, 0.0)
        + jnp.where(lane == row3 + 16, 1.0, 0.0)
    )
    for k in range(6):
        pivot_row = work[:, k : k + 1, :]
        pivot_row = pivot_row / pivot_row[:, :, k : k + 1]
        work = jnp.where(row3 == k, pivot_row, work - work[:, :, k : k + 1] * pivot_row)
    inv_cols = [jnp.broadcast_to(work[:, :, 16 + m : 17 + m], shape3) for m in range(6)]
    gf_cols = [jnp.broadcast_to(grams[:, :, 8 + m : 9 + m], shape3) for m in range(6)]

    def apply(columns, value):
        result = columns[0] * value[:, 0:1, :]
        for m in range(1, 6):
            result = result + columns[m] * value[:, m : m + 1, :]
        return result

    def flat(value):
        return value.reshape(n8, cols)

    def pair(a, b):
        return low_right(jnp.concatenate([flat(a), flat(b)], axis=0))

    def sum_rows(value):
        return jnp.sum(value, axis=0, keepdims=True)

    c0 = apply(inv_cols, coarse0)
    coarse1 = coarse0 - apply(gf_cols, c0)
    w1 = apply(inv_cols, coarse1)
    weights0 = pair(c0, w1)
    now = image[...] - bdot(low_image[...], weights0)
    y_own[0] = now[0:rows]
    y0_copies = ring(2, y_own.at[0], y_p.at[0], False)
    coarse_rows0 = now[rows:]
    image[rows:] = coarse_rows0

    def second_store(ref, digit):
        u_now[...] = v_own[0] - bdot(low_u[...], weights0)
        res0[...] = x_own[...] - bdot(low_res[...], weights0)
        ref[digit, 0 : 2 * n8, :] = coarse_rows0
        ref[digit, 6:7, :] = sum_rows(u_now[...] * y_own[0])
        ref[digit, 7:8, :] = sum_rows(res0[...] * res0[...])

    second_image = []

    def second_product():
        for copy in y0_copies:
            copy.wait_recv()
        v_own[1] = mask_sum[...] * (y_own[0] - y_p[0])
        second_image.append(swap_product(1))

    second = all_reduce(1, second_store, [second_product])
    f_coarse = second[0:n8].reshape(shape3)
    r_coarse = second[n8 : 2 * n8].reshape(shape3)
    curvature0 = second[6:7]
    norm0 = second[7:8]
    step0 = norm0 / curvature0
    step_w = apply(inv_cols, r_coarse) * step0[None]
    coarse2 = coarse1 - step0[None] * f_coarse + apply(gf_cols, step_w)
    w2 = apply(inv_cols, coarse2)

    weights1 = pair(step_w, w1 - w2)
    change = second_image[0] * step0 - bdot(low_image[...], weights1)
    y_own[1] = y_own[0] - change[0:rows]
    y1_copies = ring(3, y_own.at[1], y_p.at[1], False)

    def third_store(ref, digit):
        u_next = u_now[...] - step0 * v_own[1] + bdot(low_u[...], weights1)
        res1[...] = (
            res0[...]
            - step0 * (mask_own[...] * (y_own[0] - y_p[0]))
            + bdot(low_res[...], weights1)
        )
        ref[digit, 0:n8, :] = image[rows + n8 :] - change[rows + n8 :]
        ref[digit, 6:7, :] = sum_rows(u_next * y_own[1])
        ref[digit, 7:8, :] = sum_rows(u_next * y_own[0])
        ref[digit, 14:15, :] = sum_rows(res1[...] * res1[...])

    def wait_y1():
        for copy in y1_copies:
            copy.wait_recv()

    third = all_reduce(2, third_store, [wait_y1])
    norm1 = third[14:15]
    ratio = norm1 / norm0
    curvature1 = (
        third[6:7] + ratio * (2.0 * third[7:8]) + ratio * (ratio * curvature0)
    )
    step1 = norm1 / curvature1
    w_out = apply(inv_cols, third[0:n8].reshape(shape3) + ratio[None] * r_coarse) * step1[None]
    mult_ref[0] = step0 * res0[...] + step1 * (res1[...] + ratio * res0[...])
    jump = (y_own[1] - y_p[1]) + ratio * (y_own[0] - y_p[0])
    res_ref[0] = (
        res1[...]
        - step1 * (mask_own[...] * jump)
        + bdot(low_res[...], pair(w_out, jnp.zeros_like(w_out)))
    )
    for copy in sends:
        copy.wait_send()


def solution(mesh):
    subs = mesh.shape["sub"]
    devices = subs * mesh.shape["face"]
    plan = stage_plan(devices)

    def on_device(schur, modes, loads, sizes, contact, friction, cluster_ids, pairing):
        del pairing
        _, rows, cols = loads.shape
        clusters = subs // 8
        n8 = 8 * clusters
        vmem = pl.BlockSpec(memory_space=pltpu.VMEM)
        field = pltpu.VMEM((rows, cols), F32)
        pair = pltpu.VMEM((2, rows, cols), F32)
        slot_rows = (2 * n8, 2 * n8, n8)
        slots = [pltpu.VMEM((radix, count, cols), F32) for count in slot_rows for _, radix in plan]
        reds = 3 * sum(radix - 1 for _, radix in plan)
        tall = rows + 2 * n8
        return pl.pallas_call(
            functools.partial(kernel, subs, clusters, plan),
            out_shape=[jax.ShapeDtypeStruct(loads.shape, F32)] * 2,
            in_specs=[pl.BlockSpec(memory_space=pl.ANY)] * 7,
            out_specs=[vmem, vmem],
            scratch_shapes=[
                pltpu.VMEM((2, rows, rows), F32),
                field,
                pltpu.VMEM((6, 1, rows), F32),
                pltpu.VMEM((1, rows), jnp.int32),
                pltpu.VMEM((1, rows), jnp.int32),
                pltpu.SMEM((1, 2), jnp.int32),
                pltpu.SMEM((1,), jnp.int32),
                pltpu.VMEM((2, tall, rows), BF16),
                pltpu.VMEM((2, tall, rows), BF16),
                pltpu.VMEM((8, rows), F32),
                pltpu.VMEM((8, rows), F32),
                pltpu.VMEM((2 * n8, rows), F32),
                pltpu.VMEM((2 * n8, rows), F32),
                field,
                field,
                pair,
                pair,
                pair,
                pair,
                pltpu.VMEM((128, rows), F32),
                pltpu.VMEM((tall, 12 * n8), BF16),
                pltpu.VMEM((rows, 12 * n8), BF16),
                pltpu.VMEM((rows, 12 * n8), BF16),
                field,
                field,
                pltpu.VMEM((tall, cols), F32),
                field,
                field,
                field,
                pltpu.SemaphoreType.DMA((8,)),
                pltpu.SemaphoreType.DMA((8,)),
                pltpu.SemaphoreType.DMA((8,)),
                pltpu.SemaphoreType.DMA((3,)),
                pltpu.SemaphoreType.DMA((3,)),
                pltpu.SemaphoreType.DMA((reds,)),
                pltpu.SemaphoreType.DMA((reds,)),
                *slots,
            ],
            compiler_params=pltpu.CompilerParams(
                collective_id=0, has_side_effects=True, vmem_limit_bytes=60 * 1024 * 1024
            ),
        )(
            schur,
            modes.reshape(modes.shape[1], 1, rows),
            loads,
            sizes,
            contact,
            friction,
            cluster_ids,
        )

    placed = (
        P("sub", "face", None),
        P("sub", None, "face"),
        P("sub", "face", None),
        P("sub", "face"),
        P("sub", "face"),
        P("sub", "face"),
        P("sub"),
        P("sub", "face", None, None),
    )
    return jax.shard_map(
        on_device,
        mesh=mesh,
        in_specs=placed,
        out_specs=(P("sub", "face", None), P("sub", "face", None)),
        check_vma=False,
    )
```
